32 devices in a mesh: path: 8 (over z, y), land: 4 (over x, core).
Axes of the slice: x: 2, y: 2, z: 4, core: 2. Of those that a mesh axis runs over, the one named last changes fastest.
Arguments:
- state: float32 [50, 32768], P(None, 'path'), may hold values from -6 to 6
- next_value: float32 [32768], P('path'), may hold values from -6 to 6
- brownian: float32 [15, 32768], P(None, 'path'), may hold values from -6 to 6
- land_index: int32 [8192], P('land'), may hold values from 0 to 32767
Outputs:
- estimates: float32 [16, 32768], P(None, 'path')
The draws below stay inside these ranges and needn't reach their ends.
All inputs are finite; a program needn't handle non-finite values.
Results may differ from the reference program's by a relative error of at most 0.0002.
Values sent between devices are 32-bit elements; how exact they have to be, the bound alone decides.
No kernel may reach another device: no remote copies, remote signals or barrier semaphores. Data moves between devices by JAX's collectives and lax.ppermute only.
A program may use at most 64 MiB of HBM per device.

```python
import math
import jax
import jax.numpy as jnp
from jax import lax

D = 50
M = 8192
COLS = 16
ITERS = 2
PATHS = 32768


def touch_ends(entries, stream_key, least, largest):
    extent = entries.shape
    index_at = [jax.random.randint(jax.random.fold_in(stream_key, axis), (), 0, extent[axis]) for axis in range(len(extent))]
    entries = entries.at[tuple(index_at)].set(least)
    longest = extent.index(max(extent))
    index_at[longest] = (index_at[longest] + 1) % extent[longest]
    return entries.at[tuple(index_at)].set(largest)


def level_of(key, shape, cuts, smallest, largest):
    loudness = 1.0
    for position, shards_of in cuts:
        heights = jax.random.uniform(jax.random.fold_in(jax.random.fold_in(key, 6), position), (shards_of,), jnp.float32, smallest / len(cuts), largest / len(cuts))
        loudness = loudness * jnp.repeat(jnp.exp(heights), shape[position] // shards_of).reshape((-1,) + (1,) * (len(shape) - 1 - position))
    return loudness


def gaussian(stream_key, extent, deviation, reach, shards=(), held_as=jnp.bfloat16):
    gain = level_of(stream_key, extent, shards, -0.22, 0.18) if shards else 1.0
    result = jax.random.normal(stream_key, extent, jnp.float32) * deviation * gain
    return jnp.minimum(jnp.maximum(result, -reach), reach).astype(held_as)


def setup_inputs(seed: int = 0) -> dict:
    keys = jax.random.split(jax.random.key(seed), 5)
    state = gaussian(keys[0], (D, PATHS), 1.0, 6.0, ((1, 8),), jnp.float32)
    next_value = gaussian(keys[1], (PATHS,), 1.0, 6.0, ((0, 8),), jnp.float32)
    brownian = gaussian(keys[2], (COLS - 1, PATHS), 1.0, 6.0, ((1, 8),), jnp.float32)
    land_index = touch_ends(jax.random.randint(keys[3], (M,), 0, PATHS), jax.random.fold_in(keys[3], 1), 0, PATHS - 1).astype(jnp.int32)
    return dict(state=state, next_value=next_value, brownian=brownian, land_index=land_index)


LAMBDA_REG = 0.01

def features(rows, marks):
    cross = lax.dot_general(rows, marks, (((0,), (0,)), ((), ())), precision=lax.Precision.HIGHEST)
    dist = lax.optimization_barrier(jnp.sum(rows * rows, 0))[:, None] + lax.optimization_barrier(jnp.sum(marks * marks, 0))[None, :] - 2.0 * cross
    return jnp.exp(4.0 * (2.0 * D - jnp.maximum(dist, 0.0)) / D) / math.sqrt(M)

def forward(state, marks, coef):
    width = min(512, PATHS)
    count = PATHS // width
    blocks = jnp.moveaxis(state.reshape(D, count, width), 1, 0)

    def one(rows):
        feat = features(rows, marks)
        return lax.dot_general(coef, feat, (((1,), (1,)), ((), ())), precision=lax.Precision.HIGHEST)
    out = lax.map(one, blocks)
    return jnp.moveaxis(out, 0, 1).reshape(COLS, PATHS)

def backward(state, marks, values):
    width = min(512, PATHS)
    count = PATHS // width
    blocks = jnp.moveaxis(state.reshape(D, count, width), 1, 0)
    vblocks = jnp.moveaxis(values.reshape(COLS, count, width), 1, 0)

    def step(total, pair):
        feat = features(pair[0], marks)
        return (total + jnp.dot(pair[1], feat, precision=lax.Precision.HIGHEST), None)
    total, unused = lax.scan(step, jnp.zeros((COLS, M), jnp.float32), (blocks, vblocks))
    return total

def reference(state, next_value, brownian, land_index):
    marks = jnp.take(state, land_index.astype(jnp.int32), axis=1)
    targets = jnp.concatenate([next_value[None, :], next_value[None, :] * brownian], 0)
    rhs = backward(state, marks, targets) / PATHS
    coef = jnp.zeros_like(rhs)
    resid = rhs
    direction = rhs
    norm_now = lax.optimization_barrier(jnp.sum(resid * resid, 1))
    for step in range(ITERS):
        image = backward(state, marks, forward(state, marks, direction)) / PATHS + LAMBDA_REG * direction
        alpha = norm_now / lax.optimization_barrier(jnp.sum(direction * image, 1))
        coef = coef + alpha[:, None] * direction
        resid = resid - alpha[:, None] * image
        norm_next = lax.optimization_barrier(jnp.sum(resid * resid, 1))
        direction = resid + (norm_next / norm_now)[:, None] * direction
        norm_now = norm_next
    return forward(state, marks, coef)
```

```python
import math

import jax
import jax.numpy as jnp
from jax import lax
from jax.experimental import pallas as pl
from jax.experimental.pallas import tpu as pltpu
from jax.sharding import PartitionSpec as P

LAMBDA_REG = 0.01
LOG2E = 1.4426950408889634
DEPTH = 256
BAND = DEPTH // 4
WHOLE = pl.BlockSpec(memory_space=pltpu.VMEM)
BF16, F32 = jnp.bfloat16, jnp.float32


def pieces(x, count):
    out = []
    for unused in range(count):
        part = x.astype(BF16).astype(F32)
        out.append(part)
        x = x - part
    return out


def augment(ref, x, top, of_path):
    dims, count = x.shape
    rate = 4.0 * LOG2E / dims
    norm = -rate * jnp.sum(x * x, 0, keepdims=True)
    ones = jnp.ones((1, count), F32)
    if of_path:
        high, low = pieces(x * (2.0 * rate), 2)
        bands = (high, high, low, low)
        extra = pieces(norm + top, 3) + [ones] * 3
    else:
        high, low = pieces(x, 2)
        bands = (high, low, high, low)
        extra = [ones] * 3 + pieces(norm, 3)
    ref[...] = jnp.zeros_like(ref)
    for place, band in enumerate(bands):
        ref[place * BAND : place * BAND + dims, :] = band
    for place, row in enumerate(extra):
        ref[dims + place : dims + place + 1, :] = row


def prepare(x, top, of_path):
    count = x.shape[1]

    def kernel(x_ref, out_ref, turned_ref, full):
        augment(full, x_ref[...], top, of_path)
        step = min(512, count)
        for start in range(0, count, step):
            block = full[:, start : start + step]
            out_ref[:, start : start + step] = block.astype(BF16)
            turned_ref[start : start + step, :] = block.T.astype(BF16)

    return pl.pallas_call(
        kernel,
        in_specs=[WHOLE],
        out_specs=[WHOLE, WHOLE],
        out_shape=[
            jax.ShapeDtypeStruct((DEPTH, count), BF16),
            jax.ShapeDtypeStruct((count, DEPTH), BF16),
        ],
        scratch_shapes=[pltpu.VMEM((DEPTH, count), F32)],
        compiler_params=pltpu.CompilerParams(vmem_limit_bytes=40 * 2**20),
        name="prepare",
    )(x)


def apply_features(left, right, values, other, top):
    depth, width = left.shape[0], right.shape[1]
    rows = values.shape[0]
    tile = min(512, depth)
    span = min(1024, width)

    def kernel(left_ref, right_ref, values_ref, other_ref, out_ref):
        v = values_ref[...]
        square = jnp.sum(v * v, 1, keepdims=True)
        mixed = jnp.sum(v * other_ref[...], 1, keepdims=True)
        lane = lax.broadcasted_iota(jnp.int32, (rows, 128), 1)
        out_ref[:, width:] = jnp.where(lane < 64, square, mixed)
        out_ref[:, :width] = jnp.zeros((rows, width), F32)

        @pl.loop(0, depth // tile)
        def _(i):
            at = pl.ds(pl.multiple_of(i * tile, tile), tile)
            part = values_ref[:, at]
            part_high = part.astype(BF16)
            part_low = (part - part_high.astype(F32)).astype(BF16)
            both = jnp.concatenate([part_high, part_low], 0)
            for start in range(0, width, span):
                exponent = jnp.dot(
                    left_ref[at, :], right_ref[:, start : start + span], preferred_element_type=F32
                )
                feat = jnp.exp2(jnp.minimum(exponent, top))
                high = feat.astype(BF16)
                low = (feat - high.astype(F32)).astype(BF16)
                first = jnp.dot(both, high, preferred_element_type=F32)
                second = jnp.dot(part_high, low, preferred_element_type=F32)
                out_ref[:, start : start + span] += first[:rows] + first[rows:] + second

    return pl.pallas_call(
        kernel,
        in_specs=[WHOLE] * 4,
        out_specs=WHOLE,
        out_shape=jax.ShapeDtypeStruct((rows, width + 128), F32),
        compiler_params=pltpu.CompilerParams(vmem_limit_bytes=40 * 2**20),
        name="apply_features",
    )(left, right, values, other)


def swap(x, axis, bit):
    count = lax.axis_size(axis)
    return lax.ppermute(x, axis, [(i, i ^ bit) for i in range(count)])


def bits(axis):
    out, bit = [], 1
    while bit < lax.axis_size(axis):
        out.append(bit)
        bit *= 2
    return out


def total(x, axis):
    for bit in bits(axis):
        x = x + swap(x, axis, bit)
    return x


def total_by_halves(x, axis):
    here = lax.axis_index(axis)
    for bit in bits(axis):
        half = x.shape[1] // 2
        upper = (here & bit) != 0
        keep = jnp.where(upper, x[:, half:], x[:, :half])
        send = jnp.where(upper, x[:, :half], x[:, half:])
        x = keep + swap(send, axis, bit)
    for bit in reversed(bits(axis)):
        upper = (here & bit) != 0
        other = swap(x, axis, bit)
        x = jnp.where(
            upper, jnp.concatenate([other, x], 1), jnp.concatenate([x, other], 1)
        )
    return x


def per_device(state, next_value, brownian, land_index):
    rows = state.shape[1]
    lands = land_index.shape[0]
    paths = rows * lax.axis_size("path")
    landmarks = lands * lax.axis_size("land")
    top = 8.0 * LOG2E - 0.5 * math.log2(landmarks)

    here = lax.axis_index("path")
    owner = land_index // rows
    picked = jnp.take(state, land_index % rows, axis=1)
    picked = jnp.where((owner == here)[None, :], picked, 0.0)
    marks = total_by_halves(picked, "path")

    path_right, path_left = prepare(state, top, True)
    mark_right, mark_left = prepare(marks, top, False)
    targets = jnp.concatenate([next_value[None, :], next_value[None, :] * brownian], 0)

    def pull_back(values):
        return total(apply_features(path_left, mark_right, values, values, top), "path")

    def spread(values, other):
        return total(apply_features(mark_left, path_right, values, other, top), "land")

    rhs = pull_back(targets)[:, :lands] / paths
    spread_rhs = spread(rhs, rhs)
    first = spread_rhs[:, :rows]
    norm = spread_rhs[:, rows : rows + 1]
    back = pull_back(first)
    image = back[:, :lands] / paths + LAMBDA_REG * rhs
    alpha = norm / (back[:, lands : lands + 1] / paths + LAMBDA_REG * norm)
    resid = rhs - alpha * image
    spread_resid = spread(resid, rhs)
    norm_next = spread_resid[:, rows : rows + 1]
    mixed = spread_resid[:, rows + 64 : rows + 65]
    beta = norm_next / norm
    second = spread_resid[:, :rows] + beta * first
    squares = total(
        jnp.broadcast_to(jnp.sum(second * second, 1, keepdims=True), (second.shape[0], 128)), "path"
    )[:, :1]
    length = norm_next + 2.0 * beta * mixed + beta * beta * norm
    alpha_next = norm_next / (squares / paths + LAMBDA_REG * length)
    return alpha * first + alpha_next * second


def solution(mesh):
    in_specs = (P(None, "path"), P("path"), P(None, "path"), P("land"))
    out_specs = P(None, "path")
    return jax.shard_map(
        per_device, mesh=mesh, in_specs=in_specs, out_specs=out_specs, check_vma=False
    )
```

```python
import math

import jax
import jax.numpy as jnp
from jax import lax
from jax.experimental import pallas as pl
from jax.experimental.pallas import tpu as pltpu
from jax.sharding import PartitionSpec as P

LAMBDA_REG = 0.01
LOG2E = 1.4426950408889634
DEPTH = 256
BAND = DEPTH // 4
WHOLE = pl.BlockSpec(memory_space=pltpu.VMEM)
BF16, F32 = jnp.bfloat16, jnp.float32


def pieces(x, count):
    out = []
    for unused in range(count):
        part = x.astype(BF16).astype(F32)
        out.append(part)
        x = x - part
    return out


def split(x):
    high = x.astype(BF16)
    return high, (x - high.astype(F32)).astype(BF16)


def augment(ref, x, top, of_path):
    dims, count = x.shape
    rate = 4.0 * LOG2E / dims
    norm = -rate * jnp.sum(x * x, 0, keepdims=True)
    ones = jnp.ones((1, count), F32)
    if of_path:
        high, low = pieces(x * (2.0 * rate), 2)
        bands = (high, high, low, low)
        extra = pieces(norm + top, 3) + [ones] * 3
    else:
        high, low = pieces(x, 2)
        bands = (high, low, high, low)
        extra = [ones] * 3 + pieces(norm, 3)
    ref[...] = jnp.zeros_like(ref)
    for place, band in enumerate(bands):
        ref[place * BAND : place * BAND + dims, :] = band
    for place, row in enumerate(extra):
        ref[dims + place : dims + place + 1, :] = row


def prepare(x, top, of_path, turned):
    count = x.shape[1]
    step = min(512, count)

    def kernel(x_ref, out_ref, full):
        augment(full, x_ref[...], top, of_path)
        for start in range(0, count, step):
            block = full[:, start : start + step]
            if turned:
                out_ref[start : start + step, :] = block.T.astype(BF16)
            else:
                out_ref[:, start : start + step] = block.astype(BF16)

    return pl.pallas_call(
        kernel,
        in_specs=[WHOLE],
        out_specs=WHOLE,
        out_shape=jax.ShapeDtypeStruct((count, DEPTH) if turned else (DEPTH, count), BF16),
        scratch_shapes=[pltpu.VMEM((DEPTH, count), F32)],
        compiler_params=pltpu.CompilerParams(vmem_limit_bytes=12 * 2**20),
        name="prepare",
    )(x)


def gather_block(left, marks, values, top):
    depth, width = left.shape[0], marks.shape[1]
    rows = values.shape[0]
    tile = min(512, depth)
    span = min(1024, width)

    def kernel(left_ref, marks_ref, values_ref, out_ref, full, right):
        augment(full, marks_ref[...], top, False)
        right[...] = full[...].astype(BF16)
        out_ref[...] = jnp.zeros_like(out_ref)

        @pl.loop(0, depth // tile)
        def _(i):
            at = pl.ds(pl.multiple_of(i * tile, tile), tile)
            part_high, part_low = split(values_ref[:, at])
            both = jnp.concatenate([part_high, part_low], 0)
            for start in range(0, width, span):
                to = slice(start, start + span)
                exponent = jnp.dot(left_ref[at, :], right[:, to], preferred_element_type=F32)
                feat = jnp.exp2(jnp.minimum(exponent, top))
                high, low = split(feat)
                first = jnp.dot(both, high, preferred_element_type=F32)
                second = jnp.dot(part_high, low, preferred_element_type=F32)
                out_ref[:, to] += first[:rows] + first[rows:] + second

    return pl.pallas_call(
        kernel,
        in_specs=[WHOLE] * 3,
        out_specs=WHOLE,
        out_shape=jax.ShapeDtypeStruct((rows, width), F32),
        scratch_shapes=[pltpu.VMEM((DEPTH, width), F32), pltpu.VMEM((DEPTH, width), BF16)],
        compiler_params=pltpu.CompilerParams(vmem_limit_bytes=12 * 2**20),
        cost_estimate=pl.CostEstimate(
            flops=4 * depth * width * DEPTH,
            bytes_accessed=4 * depth * DEPTH,
            transcendentals=depth * width,
        ),
        name="gather_block",
    )(left, marks, values)


def pick(state, column):
    dims, count = state.shape
    width = column.shape[1]
    tile = min(512, count)
    span = min(1024, width)

    def kernel(state_ref, column_ref, out_ref, parts, sums):
        parts[...] = jnp.zeros_like(parts)
        for place, piece in enumerate(pieces(state_ref[...], 3)):
            parts[place * BAND : place * BAND + dims, :] = piece.astype(BF16)
        sums[...] = jnp.zeros_like(sums)
        row = lax.broadcasted_iota(jnp.int32, (tile, span), 0)

        @pl.loop(0, count // tile)
        def _(i):
            at = pl.ds(pl.multiple_of(i * tile, tile), tile)
            for start in range(0, width, span):
                to = slice(start, start + span)
                hit = row == column_ref[:, to] - i * tile
                hot = jnp.where(hit, 1.0, 0.0).astype(BF16)
                sums[:, to] += jnp.dot(parts[:, at], hot, preferred_element_type=F32)

        out_ref[...] = (sums[:dims, :] + sums[BAND : BAND + dims, :]) + sums[
            2 * BAND : 2 * BAND + dims, :
        ]

    return pl.pallas_call(
        kernel,
        in_specs=[WHOLE] * 2,
        out_specs=WHOLE,
        out_shape=jax.ShapeDtypeStruct((dims, width), F32),
        scratch_shapes=[
            pltpu.VMEM((3 * BAND, count), BF16),
            pltpu.VMEM((3 * BAND, width), F32),
        ],
        compiler_params=pltpu.CompilerParams(vmem_limit_bytes=12 * 2**20),
        name="pick",
    )(state, column)


def build_features(left, right, top):
    count, width = left.shape[0], right.shape[1]
    tile = min(256, count)

    def kernel(left_ref, right_ref, out_ref):
        @pl.loop(0, count // tile)
        def _(i):
            at = pl.ds(pl.multiple_of(i * tile, tile), tile)
            exponent = jnp.dot(left_ref[at, :], right_ref[...], preferred_element_type=F32)
            feat = jnp.exp2(jnp.minimum(exponent, top))
            high = feat.astype(BF16)
            out_ref[0, at, :] = high
            out_ref[1, at, :] = (feat - high.astype(F32)).astype(BF16)

    return pl.pallas_call(
        kernel,
        in_specs=[WHOLE] * 2,
        out_specs=WHOLE,
        out_shape=pltpu.VMEM((2, count, width), BF16),
        compiler_params=pltpu.CompilerParams(vmem_limit_bytes=8 * 2**20),
        cost_estimate=pl.CostEstimate(
            flops=2 * count * width * DEPTH,
            bytes_accessed=8 * count * width,
            transcendentals=count * width,
        ),
        name="build_features",
    )(left, right)


def spread_half(parts, half, values, other):
    rows = values.shape[0]
    count, width = parts[0].shape[1], parts[0].shape[2] // 2
    tile = min(512, count)

    def kernel(half_ref, values_ref, other_ref, *refs):
        out_ref = refs[-1]
        cols = pl.ds(pl.multiple_of(half_ref[0] * width, width), width)
        v = values_ref[...]
        square = jnp.sum(v * v, 1, keepdims=True)
        mixed = jnp.sum(v * other_ref[...], 1, keepdims=True)
        lane = lax.broadcasted_iota(jnp.int32, (rows, 128), 1)
        out_ref[:, width:] = jnp.where(lane < 64, square, mixed)
        out_ref[:, :width] = jnp.zeros((rows, width), F32)
        for place, part_ref in enumerate(refs[:-1]):
            for start in range(0, count, tile):
                at = slice(start, start + tile)
                high, low = split(values_ref[:, place * count + start : place * count + start + tile])
                both = jnp.concatenate([high, low], 0)
                first = jnp.dot(both, part_ref[0, at, cols], preferred_element_type=F32)
                second = jnp.dot(high, part_ref[1, at, cols], preferred_element_type=F32)
                out_ref[:, :width] += first[:rows] + first[rows:] + second

    return pl.pallas_call(
        kernel,
        in_specs=[pl.BlockSpec(memory_space=pltpu.SMEM)] + [WHOLE] * (2 + len(parts)),
        out_specs=WHOLE,
        out_shape=jax.ShapeDtypeStruct((rows, width + 128), F32),
        compiler_params=pltpu.CompilerParams(vmem_limit_bytes=8 * 2**20),
        name="spread_half",
    )(half, values, other, *parts)


def gather_half(parts, half, values, start_from):
    rows = values.shape[0]
    count, width = parts[0].shape[1], parts[0].shape[2] // 2
    tile = min(512, count)
    lands = count * len(parts)

    def kernel(half_ref, values_ref, from_ref, *refs):
        out_ref = refs[-1]
        cols = pl.ds(pl.multiple_of(half_ref[0] * width, width), width)
        v = values_ref[...]
        out_ref[:, lands:] = from_ref[:, lands:] + jnp.sum(v * v, 1, keepdims=True)
        high, low = split(v)
        both = jnp.concatenate([high, low], 0)
        across = (((1,), (1,)), ((), ()))
        for place, part_ref in enumerate(refs[:-1]):
            for start in range(0, count, tile):
                at = slice(start, start + tile)
                first = lax.dot_general(
                    both, part_ref[0, at, cols], across, preferred_element_type=F32
                )
                second = lax.dot_general(
                    high, part_ref[1, at, cols], across, preferred_element_type=F32
                )
                to = slice(place * count + start, place * count + start + tile)
                out_ref[:, to] = from_ref[:, to] + first[:rows] + first[rows:] + second

    return pl.pallas_call(
        kernel,
        in_specs=[pl.BlockSpec(memory_space=pltpu.SMEM)] + [WHOLE] * (2 + len(parts)),
        out_specs=WHOLE,
        out_shape=jax.ShapeDtypeStruct((rows, lands + 128), F32),
        compiler_params=pltpu.CompilerParams(vmem_limit_bytes=8 * 2**20),
        cost_estimate=pl.CostEstimate(
            flops=2 * lands * width * DEPTH,
            bytes_accessed=4 * lands * width,
            transcendentals=0,
        ),
        name="gather_half",
    )(half, values, start_from, *parts)


def swap(x, axis, bit):
    count = lax.axis_size(axis)
    return lax.ppermute(x, axis, [(i, i ^ bit) for i in range(count)])


def bits(axis):
    out, bit = [], 1
    while bit < lax.axis_size(axis):
        out.append(bit)
        bit *= 2
    return out


def total(x, axis, first=1):
    for bit in bits(axis):
        if bit >= first:
            x = x + swap(x, axis, bit)
    return x


def in_order(upper, own, other):
    return jnp.where(
        upper, jnp.concatenate([other, own], 1), jnp.concatenate([own, other], 1)
    )


def total_by_halves(x, axis, beside):
    here = lax.axis_index(axis)
    for bit in bits(axis):
        half = x.shape[1] // 2
        upper = (here & bit) != 0
        keep = jnp.where(upper, x[:, half:], x[:, :half])
        send = jnp.where(upper, x[:, :half], x[:, half:])
        other = swap(send, axis, bit)
        if bit == 1:
            keep, beside = lax.optimization_barrier((keep, beside))
        x = keep + other
    for bit in reversed(bits(axis)[1:]):
        x = in_order((here & bit) != 0, x, swap(x, axis, bit))
    return x, swap(x, axis, 1), beside


def per_device(state, next_value, brownian, land_index):
    rows = state.shape[1]
    lands = land_index.shape[0]
    half = rows // 2
    paths = rows * lax.axis_size("path")
    landmarks = lands * lax.axis_size("land")
    top = 8.0 * LOG2E - 0.5 * math.log2(landmarks)

    here = lax.axis_index("path")
    core = lax.axis_index("land") & 1
    mine, its = core[None], 1 - core[None]
    picked = pick(state, (land_index - here * rows)[None, :])
    path_right = prepare(state, top, True, False)
    path_left = prepare(state, top, True, True)
    targets = jnp.concatenate([next_value[None, :], next_value[None, :] * brownian], 0)

    marks_own, marks_other, (path_right, path_left, targets) = total_by_halves(
        picked, "path", (path_right, path_left, targets)
    )
    upper = (here & 1) != 0
    sums = [gather_block(path_left, block, targets, top) for block in (marks_own, marks_other)]
    marks = in_order(upper, marks_own, marks_other)
    rhs_part = in_order(upper, *sums)
    marks, rhs_part = lax.optimization_barrier((marks, rhs_part))
    mark_left = prepare(marks, top, False, True)
    chunk = max(lands // 4, 256)
    parts = [
        build_features(mark_left[start : start + chunk], path_right, top)
        for start in range(0, lands, chunk)
    ]
    rhs = total(rhs_part, "path") / paths

    def spread(values, other):
        theirs = spread_half(parts, its, values, other)
        ours = spread_half(parts, mine, values, other)
        ours = total(ours + swap(theirs, "land", 1), "land", 2)
        return ours[:, :half], ours[:, half:]

    first, tail = spread(rhs, rhs)
    norm = tail[:, :1]
    first_other = swap(first, "land", 1)
    back = gather_half(parts, mine, first, jnp.zeros((rhs.shape[0], lands + 128), F32))
    back = total(gather_half(parts, its, first_other, back), "path")
    image = back[:, :lands] / paths + LAMBDA_REG * rhs
    alpha = norm / (back[:, lands : lands + 1] / paths + LAMBDA_REG * norm)
    resid = rhs - alpha * image
    second, tail = spread(resid, rhs)
    norm_next, mixed = tail[:, :1], tail[:, 64:65]
    beta = norm_next / norm
    second_other = swap(second, "land", 1)
    second = second + beta * first
    second_other = second_other + beta * first_other
    squares = jnp.sum(second * second + second_other * second_other, 1, keepdims=True)
    squares = total(jnp.broadcast_to(squares, (rhs.shape[0], 128)), "path")[:, :1]
    length = norm_next + 2.0 * beta * mixed + beta * beta * norm
    alpha_next = norm_next / (squares / paths + LAMBDA_REG * length)
    return in_order(
        core != 0,
        alpha * first + alpha_next * second,
        alpha * first_other + alpha_next * second_other,
    )


def solution(mesh):
    in_specs = (P(None, "path"), P("path"), P(None, "path"), P("land"))
    out_specs = P(None, "path")
    return jax.shard_map(
        per_device, mesh=mesh, in_specs=in_specs, out_specs=out_specs, check_vma=False
    )
```

```python
import math

import jax
import jax.numpy as jnp
from jax import lax
from jax.experimental import pallas as pl
from jax.experimental.pallas import tpu as pltpu
from jax.sharding import PartitionSpec as P

LAMBDA_REG = 0.01
LOG2E = 1.4426950408889634
BAND = 64
DEPTH = 6 * BAND
WHOLE = pl.BlockSpec(memory_space=pltpu.VMEM)
BF16, F32 = jnp.bfloat16, jnp.float32


def pieces(x, count):
    out = []
    for unused in range(count):
        part = x.astype(BF16).astype(F32)
        out.append(part)
        x = x - part
    return out


def split(x):
    high = x.astype(BF16)
    return high, (x - high.astype(F32)).astype(BF16)


def split_rows(x):
    return jnp.concatenate([part.astype(BF16) for part in pieces(x, 3)], 0)


def add_rows(first, second, rows):
    small = first[2 * rows :] + (second[:rows] + second[rows:])
    return first[:rows] + (first[rows : 2 * rows] + small)


def rate_of(x):
    return 4.0 * LOG2E / x.shape[0]


def augment(ref, x, of_path):
    dims = x.shape[0]
    if of_path:
        high, middle, low = pieces(x * (2.0 * rate_of(x)), 3)
        bands = (high, high, middle, high, middle, low)
    else:
        high, middle, low = pieces(x, 3)
        bands = (high, middle, high, low, middle, high)
    ref[...] = jnp.zeros_like(ref)
    for place, band in enumerate(bands):
        ref[place * BAND : place * BAND + dims, :] = band


def prepare(x):
    count = x.shape[1]

    def kernel(x_ref, out_ref, full):
        augment(full, x_ref[...], True)
        out_ref[...] = full[...].astype(BF16)

    return pl.pallas_call(
        kernel,
        in_specs=[WHOLE],
        out_specs=WHOLE,
        out_shape=jax.ShapeDtypeStruct((DEPTH, count), BF16),
        scratch_shapes=[pltpu.VMEM((DEPTH, count), F32)],
        cost_estimate=pl.CostEstimate(
            flops=0, bytes_accessed=4 * count * DEPTH, transcendentals=0
        ),
        compiler_params=pltpu.CompilerParams(vmem_limit_bytes=8 * 2**20),
        name="prepare",
    )(x)


def gather_block(paths, norm, marks, values, top):
    depth, width = paths.shape[1], marks.shape[1]
    rows = values.shape[0]
    tile = min(512, depth)
    span = min(1024, width)

    def kernel(paths_ref, norm_ref, marks_ref, values_ref, out_ref, full, right):
        m = marks_ref[...]
        augment(full, m, False)
        mark_norm = -rate_of(m) * jnp.sum(m * m, 0, keepdims=True)
        right[...] = full[...].astype(BF16)
        out_ref[...] = jnp.zeros_like(out_ref)

        @pl.loop(0, depth // tile)
        def _(i):
            at = pl.ds(pl.multiple_of(i * tile, tile), tile)
            left = paths_ref[:, at].astype(F32).T.astype(BF16)
            norms = norm_ref[:, at].T[:, :1]
            left_rows = split_rows(values_ref[:, at])
            for start in range(0, width, span):
                to = slice(start, start + span)
                exponent = jnp.dot(left, right[:, to], preferred_element_type=F32)
                exponent = exponent + (norms + mark_norm[:, to])
                feat = jnp.exp2(jnp.minimum(exponent, top))
                high, low = split(feat)
                first = jnp.dot(left_rows, high, preferred_element_type=F32)
                second = jnp.dot(left_rows[: 2 * rows], low, preferred_element_type=F32)
                out_ref[:, to] += add_rows(first, second, rows)

    return pl.pallas_call(
        kernel,
        in_specs=[WHOLE] * 4,
        out_specs=WHOLE,
        out_shape=jax.ShapeDtypeStruct((rows, width), F32),
        scratch_shapes=[pltpu.VMEM((DEPTH, width), F32), pltpu.VMEM((DEPTH, width), BF16)],
        compiler_params=pltpu.CompilerParams(vmem_limit_bytes=8 * 2**20),
        cost_estimate=pl.CostEstimate(
            flops=4 * depth * width * DEPTH,
            bytes_accessed=4 * depth * DEPTH,
            transcendentals=depth * width,
        ),
        name="gather_block",
    )(paths, norm, marks, values)


def pick(state, column):
    dims, count = state.shape
    width = column.shape[1]
    tile = min(512, count)
    span = min(1024, width)

    def kernel(state_ref, column_ref, out_ref, parts, sums):
        parts[...] = jnp.zeros_like(parts)
        for place, piece in enumerate(pieces(state_ref[...], 3)):
            parts[place * BAND : place * BAND + dims, :] = piece.astype(BF16)
        sums[...] = jnp.zeros_like(sums)
        row = lax.broadcasted_iota(jnp.int32, (tile, span), 0)

        @pl.loop(0, count // tile)
        def _(i):
            at = pl.ds(pl.multiple_of(i * tile, tile), tile)
            for start in range(0, width, span):
                to = slice(start, start + span)
                hit = row == column_ref[:, to] - i * tile
                hot = jnp.where(hit, 1.0, 0.0).astype(BF16)
                sums[:, to] += jnp.dot(parts[:, at], hot, preferred_element_type=F32)

        out_ref[...] = (sums[:dims, :] + sums[BAND : BAND + dims, :]) + sums[
            2 * BAND : 2 * BAND + dims, :
        ]

    return pl.pallas_call(
        kernel,
        in_specs=[WHOLE] * 2,
        out_specs=WHOLE,
        out_shape=jax.ShapeDtypeStruct((dims, width), F32),
        scratch_shapes=[
            pltpu.VMEM((3 * BAND, count), BF16),
            pltpu.VMEM((3 * BAND, width), F32),
        ],
        compiler_params=pltpu.CompilerParams(vmem_limit_bytes=8 * 2**20),
        name="pick",
    )(state, column)


def build_features(marks, right, norm, top):
    count, width = marks.shape[1], right.shape[1]
    tile = min(256, count)

    def kernel(marks_ref, right_ref, norm_ref, out_ref, full, left, norms):
        m = marks_ref[...]
        augment(full, m, False)
        mark_norm = -rate_of(m) * jnp.sum(m * m, 0, keepdims=True)
        norms[...] = jnp.broadcast_to(mark_norm, (8, count)).T
        left[...] = full[...].T.astype(BF16)

        @pl.loop(0, count // tile)
        def _(i):
            at = pl.ds(pl.multiple_of(i * tile, tile), tile)
            exponent = jnp.dot(left[at, :], right_ref[...], preferred_element_type=F32)
            exponent = exponent + (norms[at, :1] + norm_ref[:1, :])
            feat = jnp.exp2(jnp.minimum(exponent, top))
            high, low = split(feat)
            out_ref[0, at, :] = high
            out_ref[1, at, :] = low

    return pl.pallas_call(
        kernel,
        in_specs=[WHOLE] * 3,
        out_specs=WHOLE,
        out_shape=pltpu.VMEM((2, count, width), BF16),
        scratch_shapes=[
            pltpu.VMEM((DEPTH, count), F32),
            pltpu.VMEM((count, DEPTH), BF16),
            pltpu.VMEM((count, 8), F32),
        ],
        compiler_params=pltpu.CompilerParams(vmem_limit_bytes=8 * 2**20),
        cost_estimate=pl.CostEstimate(
            flops=2 * count * width * DEPTH,
            bytes_accessed=8 * count * width,
            transcendentals=count * width,
        ),
        name="build_features",
    )(marks, right, norm)


def spread_half(parts, half, values, other):
    rows = values.shape[0]
    count, width = parts[0].shape[1], parts[0].shape[2] // 2
    tile = min(512, count)

    def kernel(half_ref, values_ref, other_ref, *refs):
        out_ref = refs[-1]
        cols = pl.ds(pl.multiple_of(half_ref[0] * width, width), width)
        v = values_ref[...]
        square = jnp.sum(v * v, 1, keepdims=True)
        mixed = jnp.sum(v * other_ref[...], 1, keepdims=True)
        lane = lax.broadcasted_iota(jnp.int32, (rows, 128), 1)
        out_ref[:, width:] = jnp.where(lane < 64, square, mixed)
        out_ref[:, :width] = jnp.zeros((rows, width), F32)
        for place, part_ref in enumerate(refs[:-1]):
            for start in range(0, count, tile):
                at = slice(start, start + tile)
                left_rows = split_rows(values_ref[:, place * count + start : place * count + start + tile])
                first = jnp.dot(left_rows, part_ref[0, at, cols], preferred_element_type=F32)
                second = jnp.dot(left_rows[: 2 * rows], part_ref[1, at, cols], preferred_element_type=F32)
                out_ref[:, :width] += add_rows(first, second, rows)

    return pl.pallas_call(
        kernel,
        in_specs=[pl.BlockSpec(memory_space=pltpu.SMEM)] + [WHOLE] * (2 + len(parts)),
        out_specs=WHOLE,
        out_shape=jax.ShapeDtypeStruct((rows, width + 128), F32),
        compiler_params=pltpu.CompilerParams(vmem_limit_bytes=8 * 2**20),
        name="spread_half",
    )(half, values, other, *parts)


def gather_half(parts, half, values, start_from):
    rows = values.shape[0]
    count, width = parts[0].shape[1], parts[0].shape[2] // 2
    tile = min(512, count)
    lands = count * len(parts)

    def kernel(half_ref, values_ref, from_ref, *refs):
        out_ref = refs[-1]
        cols = pl.ds(pl.multiple_of(half_ref[0] * width, width), width)
        v = values_ref[...]
        out_ref[:, lands:] = from_ref[:, lands:] + jnp.sum(v * v, 1, keepdims=True)
        left_rows = split_rows(v)
        across = (((1,), (1,)), ((), ()))
        for place, part_ref in enumerate(refs[:-1]):
            for start in range(0, count, tile):
                at = slice(start, start + tile)
                first = lax.dot_general(
                    left_rows, part_ref[0, at, cols], across, preferred_element_type=F32
                )
                second = lax.dot_general(
                    left_rows[: 2 * rows], part_ref[1, at, cols], across, preferred_element_type=F32
                )
                to = slice(place * count + start, place * count + start + tile)
                out_ref[:, to] = from_ref[:, to] + add_rows(first, second, rows)

    return pl.pallas_call(
        kernel,
        in_specs=[pl.BlockSpec(memory_space=pltpu.SMEM)] + [WHOLE] * (2 + len(parts)),
        out_specs=WHOLE,
        out_shape=jax.ShapeDtypeStruct((rows, lands + 128), F32),
        compiler_params=pltpu.CompilerParams(vmem_limit_bytes=8 * 2**20),
        cost_estimate=pl.CostEstimate(
            flops=2 * lands * width * DEPTH,
            bytes_accessed=4 * lands * width,
            transcendentals=0,
        ),
        name="gather_half",
    )(half, values, start_from, *parts)


def swap(x, axis, bit):
    count = lax.axis_size(axis)
    return lax.ppermute(x, axis, [(i, i ^ bit) for i in range(count)])


def bits(axis):
    out, bit = [], 1
    while bit < lax.axis_size(axis):
        out.append(bit)
        bit *= 2
    return out


def total(x, axis, first=1):
    for bit in bits(axis):
        if bit >= first:
            x = x + swap(x, axis, bit)
    return x


def in_order(upper, own, other):
    return jnp.where(
        upper, jnp.concatenate([other, own], 1), jnp.concatenate([own, other], 1)
    )


def total_by_halves(maker, axis, early, late):
    here = lax.axis_index(axis)
    upper = (here & 1) != 0
    send = maker(~upper)
    upper, send = lax.optimization_barrier((upper, send))
    other = swap(send, axis, 1)
    x = maker(upper) + other
    halvings = bits(axis)[1:]
    for bit in halvings:
        half = x.shape[1] // 2
        upper = (here & bit) != 0
        keep = jnp.where(upper, x[:, half:], x[:, :half])
        send = jnp.where(upper, x[:, :half], x[:, half:])
        other = swap(send, axis, bit)
        if bit == halvings[-1]:
            keep, early = lax.optimization_barrier((keep, early))
        x = keep + other
    for bit in reversed(halvings):
        other = swap(x, axis, bit)
        if bit == halvings[0]:
            x, late = lax.optimization_barrier((x, late))
        x = in_order((here & bit) != 0, x, other)
    return x, swap(x, axis, 1), early, late


def per_device(state, next_value, brownian, land_index):
    rows = state.shape[1]
    lands = land_index.shape[0]
    half = rows // 2
    paths = rows * lax.axis_size("path")
    landmarks = lands * lax.axis_size("land")
    top, scale = 0.0, math.exp(8.0) / math.sqrt(landmarks)

    here = lax.axis_index("path")
    core = lax.axis_index("land") & 1
    mine, its = core[None], 1 - core[None]
    path_right = prepare(state)
    path_norm = top - rate_of(state) * jnp.sum(state * state, 0, keepdims=True)
    path_norm = jnp.broadcast_to(path_norm, (8, rows))
    targets = jnp.concatenate([next_value[None, :], next_value[None, :] * brownian], 0)

    marks_own, marks_other, (path_right, path_norm), targets = total_by_halves(
        lambda upper: pick(
            state, jnp.where(upper, land_index[lands // 2 :], land_index[: lands // 2])[None, :] - here * rows
        ),
        "path",
        (path_right, path_norm),
        targets,
    )
    upper = (here & 1) != 0
    sums = [gather_block(path_right, path_norm, block, targets, top) for block in (marks_own, marks_other)]
    marks = in_order(upper, marks_own, marks_other)
    rhs_part = in_order(upper, *sums)
    marks, rhs_part = lax.optimization_barrier((marks, rhs_part))
    chunk = max(lands // 4, 256)
    parts = [
        build_features(marks[:, start : start + chunk], path_right, path_norm, top)
        for start in range(0, lands, chunk)
    ]
    rhs = total(rhs_part, "path") * (scale / paths)

    def spread(values, other):
        theirs = spread_half(parts, its, values, other)
        ours = spread_half(parts, mine, values, other)
        ours = total(ours + swap(theirs, "land", 1), "land", 2)
        return ours[:, :half] * scale, ours[:, half:]

    first, tail = spread(rhs, rhs)
    norm = tail[:, :1]
    first_other = swap(first, "land", 1)
    back = gather_half(parts, mine, first, jnp.zeros((rhs.shape[0], lands + 128), F32))
    back = total(gather_half(parts, its, first_other, back), "path")
    image = back[:, :lands] * (scale / paths) + LAMBDA_REG * rhs
    alpha = norm / (back[:, lands : lands + 1] / paths + LAMBDA_REG * norm)
    resid = rhs - alpha * image
    second, tail = spread(resid, rhs)
    norm_next, mixed = tail[:, :1], tail[:, 64:65]
    beta = norm_next / norm
    second_other = swap(second, "land", 1)
    second = second + beta * first
    second_other = second_other + beta * first_other
    squares = jnp.sum(second * second + second_other * second_other, 1, keepdims=True)
    squares = total(jnp.broadcast_to(squares, (rhs.shape[0], 128)), "path")[:, :1]
    length = norm_next + 2.0 * beta * mixed + beta * beta * norm
    alpha_next = norm_next / (squares / paths + LAMBDA_REG * length)
    return in_order(
        core != 0,
        alpha * first + alpha_next * second,
        alpha * first_other + alpha_next * second_other,
    )


def solution(mesh):
    in_specs = (P(None, "path"), P("path"), P(None, "path"), P("land"))
    out_specs = P(None, "path")
    return jax.shard_map(
        per_device, mesh=mesh, in_specs=in_specs, out_specs=out_specs, check_vma=False
    )
```

```python
import math

import jax
import jax.numpy as jnp
from jax import lax
from jax.experimental import pallas as pl
from jax.experimental.pallas import tpu as pltpu
from jax.sharding import PartitionSpec as P

LAMBDA_REG = 0.01
LOG2E = 1.4426950408889634
BAND = 64
DEPTH = 6 * BAND
WHOLE = pl.BlockSpec(memory_space=pltpu.VMEM)
BF16, F32 = jnp.bfloat16, jnp.float32


def pieces(x, count):
    out = []
    for unused in range(count):
        part = x.astype(BF16).astype(F32)
        out.append(part)
        x = x - part
    return out


def split(x):
    high = x.astype(BF16)
    return high, (x - high.astype(F32)).astype(BF16)


def split_rows(x):
    return jnp.concatenate([part.astype(BF16) for part in pieces(x, 3)], 0)


def add_rows(first, second, rows):
    small = first[2 * rows :] + (second[:rows] + second[rows:])
    return first[:rows] + (first[rows : 2 * rows] + small)


def augment(ref, x, top, of_path):
    dims, count = x.shape
    rate = 4.0 * LOG2E / dims
    norm = -rate * jnp.sum(x * x, 0, keepdims=True)
    ones = jnp.ones((1, count), F32)
    if of_path:
        high, middle, low = pieces(x * (2.0 * rate), 3)
        bands = (high, high, middle, high, middle, low)
        extra = pieces(norm + top, 3) + [ones] * 3
    else:
        high, middle, low = pieces(x, 3)
        bands = (high, middle, high, low, middle, high)
        extra = [ones] * 3 + pieces(norm, 3)
    ref[...] = jnp.zeros_like(ref)
    for place, band in enumerate(bands):
        ref[place * BAND : place * BAND + dims, :] = band
    for place, row in enumerate(extra):
        ref[dims + place : dims + place + 1, :] = row


def prepare(x, top):
    count = x.shape[1]

    def kernel(x_ref, out_ref, full):
        augment(full, x_ref[...], top, True)
        out_ref[...] = full[...].astype(BF16)

    return pl.pallas_call(
        kernel,
        in_specs=[WHOLE],
        out_specs=WHOLE,
        out_shape=jax.ShapeDtypeStruct((DEPTH, count), BF16),
        scratch_shapes=[pltpu.VMEM((DEPTH, count), F32)],
        cost_estimate=pl.CostEstimate(
            flops=0, bytes_accessed=4 * count * DEPTH, transcendentals=0
        ),
        compiler_params=pltpu.CompilerParams(vmem_limit_bytes=8 * 2**20),
        name="prepare",
    )(x)


def gather_block(paths, marks, values, top):
    depth, width = paths.shape[1], marks.shape[1]
    rows = values.shape[0]
    tile = min(512, depth)
    span = min(1024, width)

    def kernel(paths_ref, marks_ref, values_ref, out_ref, full, right):
        augment(full, marks_ref[...], top, False)
        right[...] = full[...].astype(BF16)
        out_ref[...] = jnp.zeros_like(out_ref)

        @pl.loop(0, depth // tile)
        def _(i):
            at = pl.ds(pl.multiple_of(i * tile, tile), tile)
            left = paths_ref[:, at].astype(F32).T.astype(BF16)
            left_rows = split_rows(values_ref[:, at])
            for start in range(0, width, span):
                to = slice(start, start + span)
                exponent = jnp.dot(left, right[:, to], preferred_element_type=F32)
                feat = jnp.exp2(jnp.minimum(exponent, top))
                high, low = split(feat)
                first = jnp.dot(left_rows, high, preferred_element_type=F32)
                second = jnp.dot(left_rows[: 2 * rows], low, preferred_element_type=F32)
                out_ref[:, to] += add_rows(first, second, rows)

    return pl.pallas_call(
        kernel,
        in_specs=[WHOLE] * 3,
        out_specs=WHOLE,
        out_shape=jax.ShapeDtypeStruct((rows, width), F32),
        scratch_shapes=[pltpu.VMEM((DEPTH, width), F32), pltpu.VMEM((DEPTH, width), BF16)],
        compiler_params=pltpu.CompilerParams(vmem_limit_bytes=8 * 2**20),
        cost_estimate=pl.CostEstimate(
            flops=4 * depth * width * DEPTH,
            bytes_accessed=4 * depth * DEPTH,
            transcendentals=depth * width,
        ),
        name="gather_block",
    )(paths, marks, values)


def pick(state, column):
    dims, count = state.shape
    width = column.shape[1]
    tile = min(512, count)
    span = min(1024, width)

    def kernel(state_ref, column_ref, out_ref, parts, sums):
        parts[...] = jnp.zeros_like(parts)
        for place, piece in enumerate(pieces(state_ref[...], 3)):
            parts[place * BAND : place * BAND + dims, :] = piece.astype(BF16)
        sums[...] = jnp.zeros_like(sums)
        row = lax.broadcasted_iota(jnp.int32, (tile, span), 0)

        @pl.loop(0, count // tile)
        def _(i):
            at = pl.ds(pl.multiple_of(i * tile, tile), tile)
            for start in range(0, width, span):
                to = slice(start, start + span)
                hit = row == column_ref[:, to] - i * tile
                hot = jnp.where(hit, 1.0, 0.0).astype(BF16)
                sums[:, to] += jnp.dot(parts[:, at], hot, preferred_element_type=F32)

        out_ref[...] = (sums[:dims, :] + sums[BAND : BAND + dims, :]) + sums[
            2 * BAND : 2 * BAND + dims, :
        ]

    return pl.pallas_call(
        kernel,
        in_specs=[WHOLE] * 2,
        out_specs=WHOLE,
        out_shape=jax.ShapeDtypeStruct((dims, width), F32),
        scratch_shapes=[
            pltpu.VMEM((3 * BAND, count), BF16),
            pltpu.VMEM((3 * BAND, width), F32),
        ],
        compiler_params=pltpu.CompilerParams(vmem_limit_bytes=8 * 2**20),
        name="pick",
    )(state, column)


def build_features(marks, right, top):
    count, width = marks.shape[1], right.shape[1]
    tile = min(256, count)

    def kernel(marks_ref, right_ref, out_ref, full, left):
        augment(full, marks_ref[...], top, False)
        left[...] = full[...].T.astype(BF16)

        @pl.loop(0, count // tile)
        def _(i):
            at = pl.ds(pl.multiple_of(i * tile, tile), tile)
            exponent = jnp.dot(left[at, :], right_ref[...], preferred_element_type=F32)
            feat = jnp.exp2(jnp.minimum(exponent, top))
            high, low = split(feat)
            out_ref[0, at, :] = high
            out_ref[1, at, :] = low

    return pl.pallas_call(
        kernel,
        in_specs=[WHOLE] * 2,
        out_specs=WHOLE,
        out_shape=pltpu.VMEM((2, count, width), BF16),
        scratch_shapes=[pltpu.VMEM((DEPTH, count), F32), pltpu.VMEM((count, DEPTH), BF16)],
        compiler_params=pltpu.CompilerParams(vmem_limit_bytes=8 * 2**20),
        cost_estimate=pl.CostEstimate(
            flops=2 * count * width * DEPTH,
            bytes_accessed=8 * count * width,
            transcendentals=count * width,
        ),
        name="build_features",
    )(marks, right)


def spread_half(parts, half, values, other):
    rows = values.shape[0]
    count, width = parts[0].shape[1], parts[0].shape[2] // 2
    tile = min(512, count)

    def kernel(half_ref, values_ref, other_ref, *refs):
        out_ref = refs[-1]
        cols = pl.ds(pl.multiple_of(half_ref[0] * width, width), width)
        v = values_ref[...]
        square = jnp.sum(v * v, 1, keepdims=True)
        mixed = jnp.sum(v * other_ref[...], 1, keepdims=True)
        lane = lax.broadcasted_iota(jnp.int32, (rows, 128), 1)
        out_ref[:, width:] = jnp.where(lane < 64, square, mixed)
        out_ref[:, :width] = jnp.zeros((rows, width), F32)
        for place, part_ref in enumerate(refs[:-1]):
            for start in range(0, count, tile):
                at = slice(start, start + tile)
                left_rows = split_rows(values_ref[:, place * count + start : place * count + start + tile])
                first = jnp.dot(left_rows, part_ref[0, at, cols], preferred_element_type=F32)
                second = jnp.dot(left_rows[: 2 * rows], part_ref[1, at, cols], preferred_element_type=F32)
                out_ref[:, :width] += add_rows(first, second, rows)

    return pl.pallas_call(
        kernel,
        in_specs=[pl.BlockSpec(memory_space=pltpu.SMEM)] + [WHOLE] * (2 + len(parts)),
        out_specs=WHOLE,
        out_shape=jax.ShapeDtypeStruct((rows, width + 128), F32),
        compiler_params=pltpu.CompilerParams(vmem_limit_bytes=8 * 2**20),
        name="spread_half",
    )(half, values, other, *parts)


def gather_half(parts, half, values, start_from):
    rows = values.shape[0]
    count, width = parts[0].shape[1], parts[0].shape[2] // 2
    tile = min(512, count)
    lands = count * len(parts)

    def kernel(half_ref, values_ref, from_ref, *refs):
        out_ref = refs[-1]
        cols = pl.ds(pl.multiple_of(half_ref[0] * width, width), width)
        v = values_ref[...]
        out_ref[:, lands:] = from_ref[:, lands:] + jnp.sum(v * v, 1, keepdims=True)
        left_rows = split_rows(v)
        across = (((1,), (1,)), ((), ()))
        for place, part_ref in enumerate(refs[:-1]):
            for start in range(0, count, tile):
                at = slice(start, start + tile)
                first = lax.dot_general(
                    left_rows, part_ref[0, at, cols], across, preferred_element_type=F32
                )
                second = lax.dot_general(
                    left_rows[: 2 * rows], part_ref[1, at, cols], across, preferred_element_type=F32
                )
                to = slice(place * count + start, place * count + start + tile)
                out_ref[:, to] = from_ref[:, to] + add_rows(first, second, rows)

    return pl.pallas_call(
        kernel,
        in_specs=[pl.BlockSpec(memory_space=pltpu.SMEM)] + [WHOLE] * (2 + len(parts)),
        out_specs=WHOLE,
        out_shape=jax.ShapeDtypeStruct((rows, lands + 128), F32),
        compiler_params=pltpu.CompilerParams(vmem_limit_bytes=8 * 2**20),
        cost_estimate=pl.CostEstimate(
            flops=2 * lands * width * DEPTH,
            bytes_accessed=4 * lands * width,
            transcendentals=0,
        ),
        name="gather_half",
    )(half, values, start_from, *parts)


def swap(x, axis, bit):
    count = lax.axis_size(axis)
    return lax.ppermute(x, axis, [(i, i ^ bit) for i in range(count)])


def bits(axis):
    out, bit = [], 1
    while bit < lax.axis_size(axis):
        out.append(bit)
        bit *= 2
    return out


def total(x, axis, first=1):
    for bit in bits(axis):
        if bit >= first:
            x = x + swap(x, axis, bit)
    return x


def in_order(upper, own, other):
    return jnp.where(
        upper, jnp.concatenate([other, own], 1), jnp.concatenate([own, other], 1)
    )


def total_by_halves(maker, axis, early, late):
    here = lax.axis_index(axis)
    upper = (here & 1) != 0
    send = maker(~upper)
    upper, send = lax.optimization_barrier((upper, send))
    other = swap(send, axis, 1)
    x = maker(upper) + other
    halvings = bits(axis)[1:]
    for bit in halvings:
        half = x.shape[1] // 2
        upper = (here & bit) != 0
        keep = jnp.where(upper, x[:, half:], x[:, :half])
        send = jnp.where(upper, x[:, :half], x[:, half:])
        other = swap(send, axis, bit)
        if bit == halvings[-1]:
            keep, early = lax.optimization_barrier((keep, early))
        x = keep + other
    for bit in reversed(halvings):
        other = swap(x, axis, bit)
        if bit == halvings[0]:
            x, late = lax.optimization_barrier((x, late))
        x = in_order((here & bit) != 0, x, other)
    return x, swap(x, axis, 1), early, late


def per_device(state, next_value, brownian, land_index):
    rows = state.shape[1]
    lands = land_index.shape[0]
    half = rows // 2
    paths = rows * lax.axis_size("path")
    landmarks = lands * lax.axis_size("land")
    top, scale = 0.0, math.exp(8.0) / math.sqrt(landmarks)

    here = lax.axis_index("path")
    core = lax.axis_index("land") & 1
    mine, its = core[None], 1 - core[None]
    path_right = prepare(state, top)
    targets = jnp.concatenate([next_value[None, :], next_value[None, :] * brownian], 0)

    marks_own, marks_other, path_right, targets = total_by_halves(
        lambda upper: pick(
            state, jnp.where(upper, land_index[lands // 2 :], land_index[: lands // 2])[None, :] - here * rows
        ),
        "path",
        path_right,
        targets,
    )
    upper = (here & 1) != 0
    sums = [gather_block(path_right, block, targets, top) for block in (marks_own, marks_other)]
    marks = in_order(upper, marks_own, marks_other)
    rhs_part = in_order(upper, *sums)
    marks, rhs_part = lax.optimization_barrier((marks, rhs_part))
    chunk = max(lands // 4, 256)
    parts = [
        build_features(marks[:, start : start + chunk], path_right, top)
        for start in range(0, lands, chunk)
    ]
    rhs = total(rhs_part, "path") * (scale / paths)

    def spread(values, other):
        theirs = spread_half(parts, its, values, other)
        ours = spread_half(parts, mine, values, other)
        ours = total(ours + swap(theirs, "land", 1), "land", 2)
        return ours[:, :half] * scale, ours[:, half:]

    first, tail = spread(rhs, rhs)
    norm = tail[:, :1]
    first_other = swap(first, "land", 1)
    back = gather_half(parts, mine, first, jnp.zeros((rhs.shape[0], lands + 128), F32))
    back = total(gather_half(parts, its, first_other, back), "path")
    image = back[:, :lands] * (scale / paths) + LAMBDA_REG * rhs
    alpha = norm / (back[:, lands : lands + 1] / paths + LAMBDA_REG * norm)
    resid = rhs - alpha * image
    second, tail = spread(resid, rhs)
    norm_next, mixed = tail[:, :1], tail[:, 64:65]
    beta = norm_next / norm
    second_other = swap(second, "land", 1)
    second = second + beta * first
    second_other = second_other + beta * first_other
    squares = jnp.sum(second * second + second_other * second_other, 1, keepdims=True)
    squares = total(jnp.broadcast_to(squares, (rhs.shape[0], 128)), "path")[:, :1]
    length = norm_next + 2.0 * beta * mixed + beta * beta * norm
    alpha_next = norm_next / (squares / paths + LAMBDA_REG * length)
    return in_order(
        core != 0,
        alpha * first + alpha_next * second,
        alpha * first_other + alpha_next * second_other,
    )


def solution(mesh):
    in_specs = (P(None, "path"), P("path"), P(None, "path"), P("land"))
    out_specs = P(None, "path")
    return jax.shard_map(
        per_device, mesh=mesh, in_specs=in_specs, out_specs=out_specs, check_vma=False
    )
```
